256 devices in a mesh: ctx: 32 (over x, y, core), tp: 8 (over z).
Axes of the slice: x: 4, y: 4, z: 8, core: 2. Of those that a mesh axis runs over, the one named last changes fastest.
Arguments:
- resp_query: bfloat16 [2048, 4096], P('ctx', 'tp'), may hold values from -16 to 16, as said below
- resp_key: bfloat16 [2048, 2048], P('ctx', 'tp'), may hold values from -6 to 6
- resp_value: bfloat16 [2048, 2048], P('ctx', 'tp'), may hold values from -6 to 6
- prompt_key: bfloat16 [16384, 2048], P('ctx', 'tp'), may hold values from -6 to 6
- prompt_value: bfloat16 [16384, 2048], P('ctx', 'tp'), may hold values from -6 to 6
- o_weight: bfloat16 [4096, 4608], P('tp'), may hold values from -0.09375 to 0.09375
- d_hidden: bfloat16 [2048, 4608], P('ctx', 'tp'), may hold values from -6 to 6
- prompt_offsets: int32 [4], replicated, may hold values from 2048 to 16384, as said below
- resp_lengths: int32 [4], replicated, may hold values from 128 to 512, as said below
Outputs:
- attn_out: bfloat16 [2048, 4096], P('ctx', 'tp')
- hidden: bfloat16 [2048, 4608], P('ctx', 'tp')
- d_query: bfloat16 [2048, 4096], P('ctx', 'tp')
- d_prompt_key: bfloat16 [16384, 2048], P('ctx', 'tp')
- d_prompt_value: bfloat16 [16384, 2048], P('ctx', 'tp')
- d_resp_key: bfloat16 [2048, 2048], P('ctx', 'tp')
- d_resp_value: bfloat16 [2048, 2048], P('ctx', 'tp')
- d_o_weight: float32 [4096, 4608], P('tp', 'ctx')
The draws below stay inside these ranges and needn't reach their ends.
Inputs may be any that keep to these rules, and one draw needn't show every extreme that they name: `resp_query`: response queries; every entry is finite. Response r follows the first prompt_offsets[r] prompt tokens; some response follows the whole prompt. Response r holds resp_lengths[r] real tokens at the start of its 512 rows; some response fills all of them.
All inputs are finite; a program needn't handle non-finite values.
Results may differ from the reference program's by a relative error of at most 0.03.
Values may be sent and summed in bfloat16 or wider, within the bound.
A program may use at most 128 MiB of HBM per device.

```python
import math
import jax
import jax.numpy as jnp
from jax import lax

D = 4608
QH = 32
KVH = 16
HD = 128
PROMPT_DEV = 512
RESPONSES = 4
RESP_LEN = 512
PROMPT = 16384
RESP = 2048
N_CTX = 32


def draw_resp_query(key, part):
    key = jax.random.fold_in(key, 11)
    noise_key, scale_key = jax.random.split(key)
    samples = jnp.clip(jax.random.normal(noise_key, (RESP, QH, HD), jnp.float32), -4.0, 4.0)
    spread = jnp.exp(jax.random.uniform(scale_key, (RESP, QH, 1), jnp.float32, math.log(0.5), math.log(1.5)))
    return (samples * spread).reshape(RESP, QH * HD).astype(jnp.bfloat16)


def draw_prompt_offsets(key, part):
    key = jax.random.fold_in(key, 23)
    offset_key, slot_key = jax.random.split(key)
    drawn = jax.random.randint(offset_key, (RESPONSES,), PROMPT // 8, PROMPT + 1, dtype=jnp.int32)
    full_slot = jax.random.randint(slot_key, (), 0, RESPONSES, dtype=jnp.int32)
    return jnp.where(jnp.arange(RESPONSES, dtype=jnp.int32) == full_slot, PROMPT, drawn).astype(jnp.int32)


def draw_resp_lengths(key, part):
    key = jax.random.fold_in(key, 37)
    length_key, slot_key = jax.random.split(key)
    drawn = jax.random.randint(length_key, (RESPONSES,), RESP_LEN // 4, RESP_LEN + 1, dtype=jnp.int32)
    full_slot = jax.random.randint(slot_key, (), 0, RESPONSES, dtype=jnp.int32)
    return jnp.where(jnp.arange(RESPONSES, dtype=jnp.int32) == full_slot, RESP_LEN, drawn).astype(jnp.int32)


def spiked(entries, key, source, target, parts, factor):
    owner, partner = [(jnp.arange(entries.shape[axis_at]) // (entries.shape[axis_at] // parts)).reshape([-1 if axis == axis_at else 1 for axis in range(entries.ndim)]) for axis_at in (source, target)]
    chosen = jax.random.permutation(key, parts)[partner]
    strong = (owner == chosen) | (owner == (partner + parts // 2) % parts)
    return jnp.where(strong, factor * entries, entries)


def levels(key, dims, pieces, low, high):
    gain = 1.0
    for dim, shards_of in pieces:
        steps = jax.random.uniform(jax.random.fold_in(jax.random.fold_in(key, 6), dim), (shards_of,), jnp.float32, low / len(pieces), high / len(pieces))
        gain = gain * jnp.repeat(jnp.exp(steps), dims[dim] // shards_of).reshape((-1,) + (1,) * (len(dims) - 1 - dim))
    return gain


def noise(rng, shape, deviation, limit, cuts=(), kind=jnp.bfloat16):
    entries = jax.random.normal(rng, shape, jnp.float32) * deviation
    if len(cuts) > 0:
        entries = levels(rng, shape, cuts, -0.22, 0.18) * entries
    return jnp.clip(entries, min=-limit, max=limit).astype(kind)


def heavy_noise(key, extent, width, bound, cuts, heavy, kind=jnp.bfloat16):
    result = width * jax.random.normal(key, extent, jnp.float32)
    if cuts:
        result = result * levels(key, extent, cuts, -0.22, 0.18)
    return jnp.clip(spiked(result, jax.random.fold_in(key, 3), *heavy), -bound, bound).astype(kind)


def setup_inputs(seed: int = 0) -> dict:
    arg_keys = jax.random.split(jax.random.key(seed), 10)
    resp_query = draw_resp_query(jax.random.fold_in(arg_keys[9], 71), 0)
    resp_key = noise(arg_keys[1], (RESP, KVH * HD), 1.0, 6.0, ((0, 32), (1, 8)))
    resp_value = noise(arg_keys[2], (RESP, KVH * HD), 1.0, 6.0, ((0, 32), (1, 8)))
    prompt_key = noise(arg_keys[3], (PROMPT, KVH * HD), 1.0, 6.0, ((0, 32), (1, 8)))
    prompt_value = noise(arg_keys[4], (PROMPT, KVH * HD), 1.0, 6.0, ((0, 32), (1, 8)))
    o_weight = noise(arg_keys[5], (QH * HD, D), (QH * HD) ** -0.5, 0.09375, ((0, 8),))
    d_hidden = heavy_noise(arg_keys[6], (RESP, D), 1.0, 6.0, ((0, 32), (1, 8)), (0, 1, 32, 2.75))
    prompt_offsets = draw_prompt_offsets(jax.random.fold_in(arg_keys[9], 71), 0)
    resp_lengths = draw_resp_lengths(jax.random.fold_in(arg_keys[9], 71), 0)
    return {"resp_query": resp_query, "resp_key": resp_key, "resp_value": resp_value, "prompt_key": prompt_key, "prompt_value": prompt_value, "o_weight": o_weight, "d_hidden": d_hidden, "prompt_offsets": prompt_offsets, "resp_lengths": resp_lengths}


SOFTCAP = 50.0
ATTN_SCALE = 144.0 ** -0.5


def response_table(row_ids, per_response):
    response_of = row_ids // RESP_LEN
    response_ids = jnp.arange(RESPONSES, dtype=jnp.int32)
    matches = response_of[:, None] == response_ids[None, :]
    return jnp.sum(jnp.where(matches, per_response[None, :], 0), axis=1).astype(jnp.int32)


def visibility(row_ids, prompt_pos, resp_rows, prompt_offsets, resp_lengths):
    response_of = row_ids // RESP_LEN
    position = row_ids % RESP_LEN
    offset_row = response_table(row_ids, prompt_offsets)
    length_row = response_table(row_ids, resp_lengths)
    key_response = resp_rows // RESP_LEN
    key_position = resp_rows % RESP_LEN
    see_prompt = (prompt_pos[None, :] >= 0) & (prompt_pos[None, :] < offset_row[:, None])
    see_own = (resp_rows[None, :] >= 0) & (key_response[None, :] == response_of[:, None])
    see_own = see_own & (key_position[None, :] <= position[:, None]) & (key_position[None, :] < length_row[:, None])
    return see_prompt | see_own


def block_scores(query_block, key_head):
    raw_score = jnp.einsum("qgd,kd->gqk", query_block.astype(jnp.float32), key_head.astype(jnp.float32)) * ATTN_SCALE
    return SOFTCAP * jnp.tanh(raw_score / SOFTCAP)


def key_order():
    block_len = PROMPT_DEV + RESP // N_CTX
    slots = jnp.arange(PROMPT + RESP, dtype=jnp.int32)
    owner = slots // block_len
    inner = slots % block_len
    return jnp.where(inner < PROMPT_DEV, owner * PROMPT_DEV + inner,
                     PROMPT + owner * (RESP // N_CTX) + inner - PROMPT_DEV).astype(jnp.int32)


def split_blocks(matrix):
    return matrix.reshape(matrix.shape[0], matrix.shape[1], N_CTX, matrix.shape[2] // N_CTX)


def head_forward(query_head, key_head, value_head, prompt_pos, resp_rows, prompt_offsets, resp_lengths):
    merged = []
    totals = []
    value_blocks = value_head.astype(jnp.float32).reshape(N_CTX, -1, HD)
    for response_index in range(RESPONSES):
        row_ids = response_index * RESP_LEN + jnp.arange(RESP_LEN, dtype=jnp.int32)
        visible = visibility(row_ids, prompt_pos, resp_rows, prompt_offsets, resp_lengths)
        query_block = query_head[response_index * RESP_LEN:(response_index + 1) * RESP_LEN]
        scores = block_scores(query_block, key_head)
        weights = jnp.where(visible[None], jnp.exp(scores), 0.0)
        row_total = jnp.sum(weights, axis=2).T
        totals.append(row_total)
        rounded = lax.optimization_barrier(weights.astype(jnp.bfloat16)).astype(jnp.float32)
        numer = jnp.einsum("gqck,ckd->cqgd", split_blocks(rounded), value_blocks)
        terms = numer / row_total[None, :, :, None]
        merged.append(jnp.sum(terms, axis=0))
    return jnp.concatenate(merged, 0), jnp.concatenate(totals, 0)


def head_backward(query_head, key_head, value_head, total_head, grad_head, delta_head,
                  prompt_pos, resp_rows, prompt_offsets, resp_lengths):
    query_grads = []
    key_grad = jnp.zeros(key_head.shape, jnp.float32)
    value_grad = jnp.zeros(value_head.shape, jnp.float32)
    key_blocks = key_head.astype(jnp.float32).reshape(N_CTX, -1, HD)
    for response_index in range(RESPONSES):
        lower = response_index * RESP_LEN
        upper = lower + RESP_LEN
        row_ids = lower + jnp.arange(RESP_LEN, dtype=jnp.int32)
        visible = visibility(row_ids, prompt_pos, resp_rows, prompt_offsets, resp_lengths)
        query_block = query_head[lower:upper]
        grad_block = grad_head[lower:upper].astype(jnp.float32)
        scores = block_scores(query_block, key_head)
        weights = jnp.where(visible[None], jnp.exp(scores), 0.0)
        probs = weights / total_head[lower:upper].T[:, :, None]
        prob_grad = jnp.einsum("qgd,kd->gqk", grad_block, value_head.astype(jnp.float32))
        capped = 1.0 - (scores / SOFTCAP) * (scores / SOFTCAP)
        score_grad = probs * (prob_grad - delta_head[lower:upper].T[:, :, None]) * capped * ATTN_SCALE
        score_grad = lax.optimization_barrier(score_grad.astype(jnp.bfloat16)).astype(jnp.float32)
        terms = jnp.einsum("gqck,ckd->cqgd", split_blocks(score_grad), key_blocks)
        query_grads.append(jnp.sum(terms, axis=0))
        key_grad = key_grad + jnp.einsum("gqk,qgd->kd", score_grad, query_block.astype(jnp.float32))
        probs_round = lax.optimization_barrier(probs.astype(jnp.bfloat16)).astype(jnp.float32)
        value_grad = value_grad + jnp.einsum("gqk,qgd->kd", probs_round, grad_block)
    return jnp.concatenate(query_grads, 0), key_grad, value_grad


def reference(resp_query, resp_key, resp_value, prompt_key, prompt_value, o_weight, d_hidden,
              prompt_offsets, resp_lengths):
    group_size = QH // KVH
    key_total = PROMPT + RESP
    block_len = PROMPT_DEV + RESP // N_CTX
    order = key_order()
    key_rows = jnp.take(jnp.concatenate([prompt_key, resp_key], 0), order, axis=0)
    value_rows = jnp.take(jnp.concatenate([prompt_value, resp_value], 0), order, axis=0)
    key_rows = key_rows.reshape(key_total, KVH, HD).transpose(1, 0, 2)
    value_rows = value_rows.reshape(key_total, KVH, HD).transpose(1, 0, 2)
    query_heads = resp_query.reshape(RESP, KVH, group_size, HD).transpose(1, 0, 2, 3)
    prompt_pos = jnp.where(order < PROMPT, order, -1).astype(jnp.int32)
    resp_rows = jnp.where(order >= PROMPT, order - PROMPT, -1).astype(jnp.int32)

    def forward_one(operands):
        return head_forward(operands[0], operands[1], operands[2], prompt_pos, resp_rows,
                            prompt_offsets, resp_lengths)

    merged, totals = lax.map(forward_one, (query_heads, key_rows, value_rows))
    merged = merged.transpose(1, 0, 2, 3).reshape(RESP, QH, HD)
    totals = totals.transpose(1, 0, 2).reshape(RESP, QH)
    all_rows = jnp.arange(RESP, dtype=jnp.int32)
    valid = all_rows % RESP_LEN < response_table(all_rows, resp_lengths)
    attn_out = jnp.where(valid[:, None, None], merged, 0.0)
    attn_out = attn_out.astype(jnp.bfloat16).reshape(RESP, QH * HD)
    hidden = jnp.dot(attn_out, o_weight, preferred_element_type=jnp.float32).astype(jnp.bfloat16)
    grad_out = jnp.dot(d_hidden, o_weight.T, preferred_element_type=jnp.float32).astype(jnp.bfloat16)
    grad_out = jnp.where(valid[:, None], grad_out, jnp.zeros_like(grad_out))
    row_delta = jnp.sum(grad_out.astype(jnp.float32).reshape(RESP, QH, HD)
                        * attn_out.astype(jnp.float32).reshape(RESP, QH, HD), axis=2)
    grad_heads = grad_out.reshape(RESP, KVH, group_size, HD).transpose(1, 0, 2, 3)
    total_heads = totals.reshape(RESP, KVH, group_size).transpose(1, 0, 2)
    delta_heads = row_delta.reshape(RESP, KVH, group_size).transpose(1, 0, 2)

    def backward_one(operands):
        return head_backward(operands[0], operands[1], operands[2], operands[3], operands[4], operands[5],
                             prompt_pos, resp_rows, prompt_offsets, resp_lengths)

    query_grad, key_grad, value_grad = lax.map(
        backward_one, (query_heads, key_rows, value_rows, total_heads, grad_heads, delta_heads))
    d_query = query_grad.transpose(1, 0, 2, 3).reshape(RESP, QH * HD).astype(jnp.bfloat16)
    key_grad = key_grad.transpose(1, 0, 2).reshape(N_CTX, block_len, KVH * HD).astype(jnp.bfloat16)
    value_grad = value_grad.transpose(1, 0, 2).reshape(N_CTX, block_len, KVH * HD).astype(jnp.bfloat16)
    d_o_weight = jnp.dot(attn_out.T, d_hidden, preferred_element_type=jnp.float32)
    return (attn_out, hidden, d_query,
            key_grad[:, :PROMPT_DEV].reshape(PROMPT, KVH * HD),
            value_grad[:, :PROMPT_DEV].reshape(PROMPT, KVH * HD),
            key_grad[:, PROMPT_DEV:].reshape(RESP, KVH * HD),
            value_grad[:, PROMPT_DEV:].reshape(RESP, KVH * HD), d_o_weight)
```

```python
import math

import jax
import jax.numpy as jnp
from jax import lax
from jax.experimental import pallas as pl
from jax.experimental.pallas import tpu as pltpu
from jax.sharding import PartitionSpec as P

F32 = jnp.float32
BF16 = jnp.bfloat16
MESH = pl.DeviceIdType.MESH

NX, NY, NZ = 4, 4, 8
CHIPS = NX * NY
PAIRS = CHIPS // 2
HD = 128
ROWS = 64
PKEYS = 1024
RKEYS = 128
KEYS = PKEYS + RKEYS
CHUNK = 256
WIDTH = 4608
ZCOLS = WIDTH // NZ
JCOLS = WIDTH // CHIPS
DCOLS = JCOLS // 2
QCOLS = 512

TANH_IN = 1.0 / 600.0
EXP_IN = 50.0 * math.log2(math.e)


def dot_nt(a, b):
    return lax.dot_general(a, b, (((1,), (1,)), ((), ())), preferred_element_type=F32)


def dot_nn(a, b):
    return lax.dot_general(a, b, (((1,), (0,)), ((), ())), preferred_element_type=F32)


def dot_tn(a, b):
    return lax.dot_general(a, b, (((0,), (0,)), ((), ())), preferred_element_type=F32)


def transpose(a):
    return jnp.swapaxes(a, 0, 1)


def kernel(
    off_ref, len_ref, q_ref, dh_ref, rk_hbm, rv_hbm, pk_hbm, pv_hbm, ow_hbm,
    attn_out, hidden_out, dq_out, dpk_out, dpv_out, drk_out, drv_out, dow_out,
    qall, doall, kbuf, vbuf, kT, vT, wbuf, gbuf, wresp, gresp,
    osend, orecv, stall, atall, dhg, dfull, dhall, ow, hp, hsend, hrecv,
    dqsend, dqrecv, dkacc, dvacc, gsend, grecv, dowsend, dowrecv, oacc, dqacc,
    q_s, q_r, do_s, do_r, o_s, o_r, st_s, st_r, at_s, at_r, dh_s, dh_r, dq_s, dq_r,
    zg_s, zg_r, h_s, h_r, kv_l, kv_s, kv_r, ow_l, g_s, g_r, dw_s, dw_r,
):
    c = lax.axis_index("ctx")
    z = lax.axis_index("tp")
    core = lax.rem(c, 2)
    chip = lax.div(c, 2)
    x = lax.div(chip, NY)
    y = lax.rem(chip, NY)
    sibling = chip * 2 + 1 - core

    def peer_chip(s):
        px = lax.rem(x + lax.div(s, NY), NX)
        py = lax.rem(y + lax.rem(s, NY), NY)
        return px * NY + py

    def back(s):
        bx = lax.rem(NX - lax.div(s, NY), NX)
        by = lax.rem(NY - lax.rem(s, NY), NY)
        return bx * NY + by

    def plane_copy(src, dst_buf, send, recv, s):
        return pltpu.make_async_remote_copy(
            src_ref=src, dst_ref=dst_buf.at[back(s)], send_sem=send.at[s], recv_sem=recv.at[back(s)],
            device_id=(peer_chip(s) * 2 + core, z), device_id_type=MESH)

    def plane_wait_recv(src, buf, send, recv, s):
        pltpu.make_async_remote_copy(
            src_ref=src, dst_ref=buf.at[s], send_sem=send.at[s], recv_sem=recv.at[s],
            device_id=(peer_chip(s) * 2 + core, z), device_id_type=MESH).wait_recv()

    def z_copy(src, dst, send, recv, dz):
        return pltpu.make_async_remote_copy(
            src_ref=src, dst_ref=dst, send_sem=send.at[dz], recv_sem=recv.at[z],
            device_id=(c, lax.rem(z + dz, NZ)), device_id_type=MESH)

    own_p = pl.multiple_of(core * 512, 512)
    own_r = pl.multiple_of(PKEYS + core * ROWS, ROWS)

    def kv_pieces():
        pieces = []
        for h in range(2):
            cols = pl.ds(HD * h, HD)
            pieces.append((pk_hbm.at[:, cols], kbuf.at[h, pl.ds(own_p, 512)]))
            pieces.append((pv_hbm.at[:, cols], vbuf.at[h, pl.ds(own_p, 512)]))
            pieces.append((rk_hbm.at[:, cols], kbuf.at[h, pl.ds(own_r, ROWS)]))
            pieces.append((rv_hbm.at[:, cols], vbuf.at[h, pl.ds(own_r, ROWS)]))
        return pieces

    sib_p = pl.multiple_of(512 - core * 512, 512)
    sib_r = pl.multiple_of(PKEYS + ROWS - core * ROWS, ROWS)

    def kv_landing():
        places = []
        for h in range(2):
            places.append(kbuf.at[h, pl.ds(sib_p, 512)])
            places.append(vbuf.at[h, pl.ds(sib_p, 512)])
            places.append(kbuf.at[h, pl.ds(sib_r, ROWS)])
            places.append(vbuf.at[h, pl.ds(sib_r, ROWS)])
        return places

    for n, (src, dst) in enumerate(kv_pieces()):
        pltpu.make_async_copy(src, dst, kv_l.at[n]).start()
    ow_load = pltpu.make_async_copy(ow_hbm, ow, ow_l)
    ow_load.start()

    for h in range(2):
        for g in range(2):
            qall[0, h, g * ROWS:(g + 1) * ROWS, :] = q_ref[:, (2 * h + g) * HD:(2 * h + g + 1) * HD]
    dh_own = dh_ref[...].astype(F32)
    for half in range(2):
        dhg[2 * z + half] = dh_own[:, half * JCOLS:(half + 1) * JCOLS].astype(BF16)

    barrier = pltpu.get_barrier_semaphore()

    def greet_plane(s, carry):
        pl.semaphore_signal(barrier, inc=1, device_id=(peer_chip(s) * 2 + core, z), device_id_type=MESH)
        return carry

    def greet_z(dz, carry):
        pl.semaphore_signal(barrier, inc=1, device_id=(c, lax.rem(z + dz, NZ)), device_id_type=MESH)
        return carry

    lax.fori_loop(1, CHIPS, greet_plane, 0)
    lax.fori_loop(1, NZ, greet_z, 0)
    pl.semaphore_signal(barrier, inc=1, device_id=(sibling, z), device_id_type=MESH)
    pl.semaphore_wait(barrier, CHIPS - 1 + NZ - 1 + 1)

    for n, (src, dst) in enumerate(kv_pieces()):
        pltpu.make_async_remote_copy(
            src_ref=src, dst_ref=dst, send_sem=kv_s.at[n], recv_sem=kv_r.at[n],
            device_id=(sibling, z), device_id_type=MESH).start()

    def send_q(s, carry):
        plane_copy(qall.at[0], qall, q_s, q_r, s).start()
        return carry

    lax.fori_loop(1, CHIPS, send_q, 0)

    def send_dh(dz, carry):
        block = dhg.at[pl.ds(2 * z, 2)]
        z_copy(block, block, zg_s, zg_r, dz).start()
        return carry

    lax.fori_loop(1, NZ, send_dh, 0)

    dkacc[...] = jnp.zeros_like(dkacc)
    dvacc[...] = jnp.zeros_like(dvacc)
    for n, (src, dst) in enumerate(kv_pieces()):
        pltpu.make_async_copy(src, dst, kv_l.at[n]).wait()
    for n, dst in enumerate(kv_landing()):
        pltpu.make_async_remote_copy(
            src_ref=dst, dst_ref=dst, send_sem=kv_s.at[n], recv_sem=kv_r.at[n],
            device_id=(sibling, z), device_id_type=MESH).wait_recv()
    for h in range(2):
        vT[h, HD:, :] = jnp.ones((16, KEYS), BF16)
        for n in range(KEYS // HD):
            rows = pl.ds(n * HD, HD)
            kT[h, :, rows] = transpose(kbuf[h, rows, :])
            vT[h, 0:HD, rows] = transpose(vbuf[h, rows, :])

    sub = lax.broadcasted_iota(jnp.int32, (CHUNK, 2 * HD), 0)

    def weigh(s, mask):
        t = jnp.tanh(s * TANH_IN)
        w = jnp.exp2(t * EXP_IN)
        w = jnp.where(mask, w, 0.0)
        return w.astype(BF16), (w * (1.0 - t * t)).astype(BF16)

    def emit_o(i, h, acc):
        tot = acc[HD:, :]
        rest = tot - tot.astype(BF16).astype(F32)
        row = lax.broadcasted_iota(jnp.int32, tot.shape, 0)
        tail = jnp.where(row < 8, tot, rest).astype(BF16)
        head = acc[:HD, :].astype(BF16)
        for e in range(2):
            lanes = slice(e * HD, (e + 1) * HD)
            osend[2 * i + e, h, 0:HD, :] = head[:, lanes]
            osend[2 * i + e, h, HD:, :] = tail[:, lanes]

    def wait_q(s):
        plane_wait_recv(qall.at[0], qall, q_s, q_r, s)

    def send_o(s):
        plane_copy(osend.at[s], orecv, o_s, o_r, s).start()

    def forward_step(i, carry):
        @pl.when(i > 0)
        def _():
            wait_q(2 * i)

        wait_q(2 * i + 1)
        limit = off_ref[lax.rem(x + lax.div(i, 2), NX)] - chip * PKEYS
        for h in range(2):
            q2 = qall[pl.ds(2 * i, 2), h].reshape(2 * HD, HD)
            acc = jnp.zeros((HD + 16, 2 * HD), F32)
            for n in range(PKEYS // CHUNK):
                rows = slice(n * CHUNK, (n + 1) * CHUNK)
                wb, gb = weigh(dot_nt(kbuf[h, rows, :], q2), sub < limit - n * CHUNK)
                wbuf[i, h, rows, :] = wb
                gbuf[i, h, rows, :] = gb
                acc = acc + dot_nn(vT[h, :, rows], wb)
            oacc[h] = acc

        @pl.when(i < 2)
        def _():
            length = len_ref[x]
            lane = lax.broadcasted_iota(jnp.int32, (RKEYS, 2 * HD), 1)
            key = lax.broadcasted_iota(jnp.int32, (RKEYS, 2 * HD), 0) + y * RKEYS
            first = lax.rem(y + 2 * i, NY) * RKEYS + core * ROWS
            second = lax.rem(y + 2 * i + 1, NY) * RKEYS + core * ROWS
            row = lax.rem(lane, ROWS) + jnp.where(lane < HD, first, second)
            mask = (key <= row) & (key < length)
            for h in range(2):
                q2 = qall[pl.ds(2 * i, 2), h].reshape(2 * HD, HD)
                wb, gb = weigh(dot_nt(kbuf[h, PKEYS:, :], q2), mask)
                wresp[i, h] = wb
                gresp[i, h] = gb
                oacc[h] = oacc[h] + dot_nn(vT[h, :, PKEYS:], wb)

        for h in range(2):
            emit_o(i, h, oacc[h])

        @pl.when(i > 0)
        def _():
            send_o(2 * i)

        send_o(2 * i + 1)
        return carry

    lax.fori_loop(0, PAIRS, forward_step, 0)

    def wait_dh(dz, carry):
        src = lax.rem(z + dz, NZ)
        block = dhg.at[pl.ds(2 * src, 2)]
        pltpu.make_async_remote_copy(
            src_ref=block, dst_ref=block, send_sem=zg_s.at[dz], recv_sem=zg_r.at[src],
            device_id=(c, src), device_id_type=MESH).wait_recv()
        return carry

    lax.fori_loop(1, NZ, wait_dh, 0)

    def send_dh2(s, carry):
        plane_copy(dhg.at[peer_chip(s)], dhall, dh_s, dh_r, s).start()
        return carry

    for j in range(CHIPS):
        dfull[:, j * JCOLS:(j + 1) * JCOLS] = dhg[j].astype(F32)
    ow_load.wait()
    position = y * RKEYS + core * ROWS
    grad = dot_nt(dfull[...].astype(BF16), ow[...])
    row_at = lax.broadcasted_iota(jnp.int32, (ROWS, QCOLS), 0) + position
    grad = jnp.where(row_at < len_ref[x], grad, 0.0).astype(BF16)
    for h in range(2):
        for g in range(2):
            doall[0, h, g * ROWS:(g + 1) * ROWS, :] = grad[:, (2 * h + g) * HD:(2 * h + g + 1) * HD]

    def send_do(s, carry):
        plane_copy(doall.at[0], doall, do_s, do_r, s).start()
        return carry

    lax.fori_loop(1, CHIPS, send_do, 0)

    def merge(s, total):
        plane_wait_recv(osend.at[s], orecv, o_s, o_r, s)
        return total + orecv[s].astype(F32)

    merged = lax.fori_loop(1, CHIPS, merge, osend[0].astype(F32))
    lane = lax.broadcasted_iota(jnp.int32, (HD, HD), 1)
    valid = lax.rem(lane, ROWS) + position < len_ref[x]
    stall[0] = jnp.zeros((8, HD), F32)
    for h in range(2):
        total = merged[h, HD:HD + 1, :] + merged[h, HD + 8:HD + 9, :]
        inv = 1.0 / total
        own = jnp.where(valid, merged[h, 0:HD, :] * inv, 0.0).astype(BF16).astype(F32)
        grad_t = transpose(doall[0, h].astype(F32))
        delta = jnp.sum(own * grad_t, axis=0, keepdims=True)
        stall[0, 2 * h:2 * h + 1, :] = inv
        stall[0, 2 * h + 1:2 * h + 2, :] = delta * inv
        rows_first = transpose(own)
        for g in range(2):
            atall[0, :, (2 * h + g) * HD:(2 * h + g + 1) * HD] = rows_first[g * ROWS:(g + 1) * ROWS, :].astype(BF16)

    def send_st(s, carry):
        plane_copy(stall.at[0], stall, st_s, st_r, s).start()
        return carry

    def send_at(s, carry):
        plane_copy(atall.at[0], atall, at_s, at_r, s).start()
        return carry

    lax.fori_loop(1, CHIPS, send_st, 0)
    lax.fori_loop(1, CHIPS, send_at, 0)
    lax.fori_loop(1, CHIPS, send_dh2, 0)
    attn_out[...] = atall[0]

    hp[...] = dot_nn(atall[0], ow[...])
    for n in range(NZ):
        hsend[n] = hp[:, n * ZCOLS:(n + 1) * ZCOLS].astype(BF16)

    def send_h(dz, carry):
        z_copy(hsend.at[lax.rem(z + dz, NZ)], hrecv.at[z], h_s, h_r, dz).start()
        return carry

    lax.fori_loop(1, NZ, send_h, 0)

    def send_dq(s):
        plane_copy(dqsend.at[s], dqrecv, dq_s, dq_r, s).start()

    def wait_stats(s):
        plane_wait_recv(doall.at[0], doall, do_s, do_r, s)
        plane_wait_recv(stall.at[0], stall, st_s, st_r, s)

    def scaled_grad(i, h):
        parts, deltas = [], []
        for e in range(2):
            inv = stall[2 * i + e, 2 * h:2 * h + 1, :]
            inv = transpose(jnp.broadcast_to(inv, (HD, HD)))
            parts.append((doall[2 * i + e, h].astype(F32) * inv).astype(BF16))
            deltas.append(stall[2 * i + e, 2 * h + 1:2 * h + 2, :])
        return jnp.concatenate(parts, axis=0), jnp.concatenate(deltas, axis=1)

    def back_chunk(h, rows, wb, gb, q2, do2, delta):
        dp = dot_nt(vbuf[h, rows, :], do2)
        ds = (gb.astype(F32) * (dp - delta)).astype(BF16)
        dkacc[h, rows, :] += dot_nn(ds, q2)
        dvacc[h, rows, :] += dot_nn(wb, do2)
        return dot_nn(kT[h, :, rows], ds)

    def emit_dq(i, h, acc):
        for e in range(2):
            dqsend[2 * i + e, h] = acc[:, e * HD:(e + 1) * HD].astype(BF16)

    def backward_step(i, carry):
        @pl.when(i > 0)
        def _():
            wait_stats(2 * i)

        wait_stats(2 * i + 1)
        for h in range(2):
            q2 = qall[pl.ds(2 * i, 2), h].reshape(2 * HD, HD)
            do2, delta = scaled_grad(i, h)
            acc = jnp.zeros((HD, 2 * HD), F32)
            for n in range(PKEYS // CHUNK):
                rows = slice(n * CHUNK, (n + 1) * CHUNK)
                acc = acc + back_chunk(h, rows, wbuf[i, h, rows, :], gbuf[i, h, rows, :], q2, do2, delta)
            dqacc[h] = acc

        @pl.when(i < 2)
        def _():
            for h in range(2):
                q2 = qall[pl.ds(2 * i, 2), h].reshape(2 * HD, HD)
                do2, delta = scaled_grad(i, h)
                dqacc[h] = dqacc[h] + back_chunk(
                    h, slice(PKEYS, KEYS), wresp[i, h], gresp[i, h], q2, do2, delta)

        for h in range(2):
            emit_dq(i, h, dqacc[h])

        @pl.when(i > 0)
        def _():
            send_dq(2 * i)

        send_dq(2 * i + 1)
        return carry

    lax.fori_loop(0, PAIRS, backward_step, 0)

    def grad_swap(n):
        return pltpu.make_async_remote_copy(
            src_ref=gsend.at[n], dst_ref=grecv.at[n], send_sem=g_s.at[n], recv_sem=g_r.at[n],
            device_id=(sibling, z), device_id_type=MESH)

    for n, (acc, scale) in enumerate(((dkacc, 1.0 / 12.0), (dvacc, 1.0))):
        for h in range(2):
            gsend[2 * n + h, 0:512, :] = (acc[h, pl.ds(sib_p, 512), :] * scale).astype(BF16)
            gsend[2 * n + h, 512:, :] = (acc[h, pl.ds(sib_r, ROWS), :] * scale).astype(BF16)
            grad_swap(2 * n + h).start()

    dhall[0] = dhg[chip]

    def wait_proj(s, carry):
        plane_wait_recv(atall.at[0], atall, at_s, at_r, s)
        plane_wait_recv(dhall.at[0], dhall, dh_s, dh_r, s)
        return carry

    lax.fori_loop(1, CHIPS, wait_proj, 0)
    features = dhall[...].reshape(CHIPS * ROWS, JCOLS)
    halves = []
    for n in range(QCOLS // HD):
        rows = slice(n * HD, (n + 1) * HD)
        part = dot_tn(atall[:, :, rows].reshape(CHIPS * ROWS, HD), features)
        low, high = part[:, :DCOLS], part[:, DCOLS:]
        dowsend[rows, :] = jnp.where(core == 0, high, low)
        dow_out[rows, :] = jnp.where(core == 0, low, high)
    dow_swap = pltpu.make_async_remote_copy(
        src_ref=dowsend, dst_ref=dowrecv, send_sem=dw_s, recv_sem=dw_r,
        device_id=(sibling, z), device_id_type=MESH)
    dow_swap.start()

    def add_hidden(dz, total):
        src = lax.rem(z + dz, NZ)
        pltpu.make_async_remote_copy(
            src_ref=hsend.at[src], dst_ref=hrecv.at[src], send_sem=h_s.at[dz], recv_sem=h_r.at[src],
            device_id=(c, src), device_id_type=MESH).wait_recv()
        return total + hrecv[src].astype(F32)

    hidden_out[...] = lax.fori_loop(1, NZ, add_hidden, hsend[z].astype(F32)).astype(BF16)

    for n, (acc, scale, prompt_out, resp_out) in enumerate(
        ((dkacc, 1.0 / 12.0, dpk_out, drk_out), (dvacc, 1.0, dpv_out, drv_out))):
        for h in range(2):
            grad_swap(2 * n + h).wait()
            cols = slice(h * HD, (h + 1) * HD)
            prompt_out[:, cols] = (
                acc[h, pl.ds(own_p, 512), :] * scale + grecv[2 * n + h, 0:512, :].astype(F32)).astype(BF16)
            resp_out[:, cols] = (
                acc[h, pl.ds(own_r, ROWS), :] * scale + grecv[2 * n + h, 512:, :].astype(F32)).astype(BF16)

    def add_dq(s, total):
        plane_wait_recv(dqsend.at[s], dqrecv, dq_s, dq_r, s)
        return total + dqrecv[s].astype(F32)

    query_grad = lax.fori_loop(1, CHIPS, add_dq, dqsend[0].astype(F32))
    for h in range(2):
        rows_first = transpose(query_grad[h] * (1.0 / 12.0)).astype(BF16)
        for g in range(2):
            dq_out[:, (2 * h + g) * HD:(2 * h + g + 1) * HD] = rows_first[g * ROWS:(g + 1) * ROWS, :]

    dow_swap.wait()
    dow_out[...] += dowrecv[...]

    def finish(s, carry):
        plane_copy(qall.at[0], qall, q_s, q_r, s).wait_send()
        plane_copy(doall.at[0], doall, do_s, do_r, s).wait_send()
        plane_copy(osend.at[s], orecv, o_s, o_r, s).wait_send()
        plane_copy(stall.at[0], stall, st_s, st_r, s).wait_send()
        plane_copy(atall.at[0], atall, at_s, at_r, s).wait_send()
        plane_copy(dhg.at[peer_chip(s)], dhall, dh_s, dh_r, s).wait_send()
        plane_copy(dqsend.at[s], dqrecv, dq_s, dq_r, s).wait_send()
        return carry

    lax.fori_loop(1, CHIPS, finish, 0)

    def finish_z(dz, carry):
        block = dhg.at[pl.ds(2 * z, 2)]
        z_copy(block, block, zg_s, zg_r, dz).wait_send()
        z_copy(hsend.at[lax.rem(z + dz, NZ)], hrecv.at[z], h_s, h_r, dz).wait_send()
        return carry

    lax.fori_loop(1, NZ, finish_z, 0)
    for n, (src, dst) in enumerate(kv_pieces()):
        pltpu.make_async_remote_copy(
            src_ref=src, dst_ref=dst, send_sem=kv_s.at[n], recv_sem=kv_r.at[n],
            device_id=(sibling, z), device_id_type=MESH).wait_send()


def per_device(resp_query, resp_key, resp_value, prompt_key, prompt_value, o_weight, d_hidden,
               prompt_offsets, resp_lengths):
    smem = pl.BlockSpec(memory_space=pltpu.SMEM)
    vmem = pl.BlockSpec(memory_space=pltpu.VMEM)
    hbm = pl.BlockSpec(memory_space=pl.ANY)
    shape = jax.ShapeDtypeStruct
    sems = pltpu.SemaphoreType.DMA
    return pl.pallas_call(
        kernel,
        out_shape=(
            shape((ROWS, QCOLS), BF16), shape((ROWS, ZCOLS), BF16), shape((ROWS, QCOLS), BF16),
            shape((512, 2 * HD), BF16), shape((512, 2 * HD), BF16),
            shape((ROWS, 2 * HD), BF16), shape((ROWS, 2 * HD), BF16), shape((QCOLS, DCOLS), F32)),
        in_specs=[smem, smem, vmem, vmem, hbm, hbm, hbm, hbm, hbm],
        out_specs=[vmem] * 8,
        scratch_shapes=[
            pltpu.VMEM((CHIPS, 2, HD, HD), BF16),
            pltpu.VMEM((CHIPS, 2, HD, HD), BF16),
            pltpu.VMEM((2, KEYS, HD), BF16),
            pltpu.VMEM((2, KEYS, HD), BF16),
            pltpu.VMEM((2, HD, KEYS), BF16),
            pltpu.VMEM((2, HD + 16, KEYS), BF16),
            pltpu.VMEM((PAIRS, 2, PKEYS, 2 * HD), BF16),
            pltpu.VMEM((PAIRS, 2, PKEYS, 2 * HD), BF16),
            pltpu.VMEM((2, 2, RKEYS, 2 * HD), BF16),
            pltpu.VMEM((2, 2, RKEYS, 2 * HD), BF16),
            pltpu.VMEM((CHIPS, 2, HD + 16, HD), BF16),
            pltpu.VMEM((CHIPS, 2, HD + 16, HD), BF16),
            pltpu.VMEM((CHIPS, 8, HD), F32),
            pltpu.VMEM((CHIPS, ROWS, QCOLS), BF16),
            pltpu.VMEM((CHIPS, ROWS, JCOLS), BF16),
            pltpu.VMEM((ROWS, WIDTH), F32),
            pltpu.VMEM((CHIPS, ROWS, JCOLS), BF16),
            pltpu.VMEM((QCOLS, WIDTH), BF16),
            pltpu.VMEM((ROWS, WIDTH), F32),
            pltpu.VMEM((NZ, ROWS, ZCOLS), BF16),
            pltpu.VMEM((NZ, ROWS, ZCOLS), BF16),
            pltpu.VMEM((CHIPS, 2, HD, HD), BF16),
            pltpu.VMEM((CHIPS, 2, HD, HD), BF16),
            pltpu.VMEM((2, KEYS, HD), F32),
            pltpu.VMEM((2, KEYS, HD), F32),
            pltpu.VMEM((4, KEYS // 2, HD), BF16),
            pltpu.VMEM((4, KEYS // 2, HD), BF16),
            pltpu.VMEM((QCOLS, DCOLS), F32),
            pltpu.VMEM((QCOLS, DCOLS), F32),
            pltpu.VMEM((2, HD + 16, 2 * HD), F32),
            pltpu.VMEM((2, HD, 2 * HD), F32),
        ] + [sems((CHIPS,))] * 14 + [sems((NZ,))] * 4 + [
            sems((8,)), sems((8,)), sems((8,)), sems, sems((4,)), sems((4,)), sems, sems],
        compiler_params=pltpu.CompilerParams(
            collective_id=0, has_side_effects=True, vmem_limit_bytes=56 * 1024 * 1024),
        cost_estimate=pl.CostEstimate(flops=10 ** 10, bytes_accessed=10 ** 7, transcendentals=10 ** 7),
    )(prompt_offsets, resp_lengths, resp_query, d_hidden, resp_key, resp_value, prompt_key, prompt_value, o_weight)


def solution(mesh):
    both = P("ctx", "tp")
    return jax.shard_map(
        per_device, mesh=mesh,
        in_specs=(both, both, both, both, both, P("tp", None), both, P(), P()),
        out_specs=(both, both, both, both, both, both, both, P("tp", "ctx")),
        check_vma=False)
```

```python
import math

import jax
import jax.numpy as jnp
from jax import lax
from jax.experimental import pallas as pl
from jax.experimental.pallas import tpu as pltpu
from jax.sharding import PartitionSpec as P

F32 = jnp.float32
BF16 = jnp.bfloat16
MESH = pl.DeviceIdType.MESH

NX, NY, NZ = 4, 4, 8
CHIPS = NX * NY
PAIRS = CHIPS // 2
HD = 128
ROWS = 64
PKEYS = 1024
RKEYS = 128
KEYS = PKEYS + RKEYS
CHUNK = 256
WIDTH = 4608
ZCOLS = WIDTH // NZ
JCOLS = WIDTH // CHIPS
DCOLS = JCOLS // 2
QCOLS = 512

TANH_IN = 1.0 / 600.0
EXP_IN = 50.0 * math.log2(math.e)


def dot_nt(a, b):
    return lax.dot_general(a, b, (((1,), (1,)), ((), ())), preferred_element_type=F32)


def dot_nn(a, b):
    return lax.dot_general(a, b, (((1,), (0,)), ((), ())), preferred_element_type=F32)


def dot_tn(a, b):
    return lax.dot_general(a, b, (((0,), (0,)), ((), ())), preferred_element_type=F32)


def transpose(a):
    return jnp.swapaxes(a, 0, 1)


def kernel(
    off_ref, len_ref, q_hbm, dh_hbm, rk_hbm, rv_hbm, pk_hbm, pv_hbm, ow_hbm,
    attn_out, hidden_out, dq_out, dpk_out, dpv_out, drk_out, drv_out, dow_out,
    attn_vm, hidden_vm, dq_vm, dpk_vm, dpv_vm, drk_vm, drv_vm, dow_vm,
    qall, doall, kbuf, vbuf, kT, vT, wbuf, gbuf, wresp, gresp,
    osend, orecv, osum, olast, stall, atall, dhg, dfull, dhall, ow, hp, hsend, hrecv,
    dqsend, dqrecv, dqsum, dqlast, dkacc, dvacc, gsend, grecv, dowsend, dowrecv, oacc, dqacc, dhown,
    q_s, q_r, do_s, do_r, at_s, at_r, dh_s, dh_r,
    o1_s, o1_r, o2_s, o2_r, dq1_s, dq1_r, dq2_s, dq2_r, st_s, st_r,
    zu_s, zd_s, zg_r, h_s, h_r, q_l, dh_l, kv_l, kv_s, kv_r, ow_l, g_s, g_r, dw_s, dw_r, out_l,
):
    staged = (attn_vm, hidden_vm, dq_vm, dpk_vm, dpv_vm, drk_vm, drv_vm, dow_vm)
    results = (attn_out, hidden_out, dq_out, dpk_out, dpv_out, drk_out, drv_out, dow_out)

    def leaving(n):
        return pltpu.make_async_copy(staged[n], results[n], out_l.at[n])

    def leave(n):
        leaving(n).start()

    c = lax.axis_index("ctx")
    z = lax.axis_index("tp")
    core = lax.rem(c, 2)
    chip = lax.div(c, 2)
    x = lax.div(chip, NY)
    y = lax.rem(chip, NY)
    sibling = chip * 2 + 1 - core

    xs = [lax.rem(x + d, NX) for d in range(NX)]
    ys = [lax.rem(y + d, NY) for d in range(NY)]

    def at(dx, dy):
        px = xs[dx] if isinstance(dx, int) else lax.rem(x + dx, NX)
        py = ys[dy] if isinstance(dy, int) else lax.rem(y + dy, NY)
        return (px * NY + py) * 2 + core, z

    def place(h, m, n):
        return at(m, n) if h == 0 else at(n, m)

    def inverse(n):
        return (NX - n) % NX if isinstance(n, int) else lax.rem(NX - n, NX)

    def remote(src, dst, send, recv, device):
        return pltpu.make_async_remote_copy(
            src_ref=src, dst_ref=dst, send_sem=send, recv_sem=recv, device_id=device, device_id_type=MESH)

    def pass_first(buf, send, recv, h, way):
        to = NY * inverse(way)
        return remote(buf.at[h, 0], buf.at[h, to], send, recv.at[h, to], place(h, way, 0))

    def pass_second(buf, send, recv, h, m, way):
        to = NY * m + inverse(way)
        return remote(buf.at[h, NY * m], buf.at[h, to], send, recv.at[h, to], place(h, 0, way))

    def arrived(buf, send, recv, h, slot):
        remote(buf.at[h, 0], buf.at[h, slot], send, recv.at[h, slot], (sibling, z)).wait_recv()

    def gather(buf, send, recv, stage):
        if stage:
            for h in range(2):
                arrived(buf, send, recv, h, NY * stage)
        else:
            for way in (2, 1, 3):
                for h in range(2):
                    pass_first(buf, send, recv, h, way).start()
        for way in (2, 1, 3):
            for h in range(2):
                pass_second(buf, send, recv, h, stage, way).start()

    def gather_sent(buf, send, recv):
        blocks = buf.at[:, pl.ds(1, CHIPS - 1)]
        remote(blocks, blocks, send, recv.at[0, 0], (sibling, z)).wait_send()

    def sum_first(src, first, send, recv, h, m):
        return remote(src.at[h, m], first.at[h, inverse(m)], send, recv.at[h, inverse(m)], place(h, m, 0))

    def sum_second(mid, last, send, recv, h, n):
        return remote(mid.at[h, n], last.at[h, inverse(n)], send, recv.at[h, inverse(n)], place(h, 0, n))

    def sum_arrived(buf, send, recv, h, m):
        remote(buf.at[h, m], buf.at[h, m], send, recv.at[h, m], place(h, m, 0)).wait_recv()

    def sum_sent(src, mid, send1, recv1, send2, recv2):
        for buf, send, recv in ((src, send1, recv1), (mid, send2, recv2)):
            blocks = buf.at[:, pl.ds(1, NX - 1)]
            remote(blocks, blocks, send, recv.at[0, 0], (sibling, z)).wait_send()

    def z_copy(src, dst, send, recv, dz):
        return remote(src, dst, send.at[dz], recv.at[z], (c, lax.rem(z + dz, NZ)))

    own_p = pl.multiple_of(core * 512, 512)
    own_r = pl.multiple_of(PKEYS + core * ROWS, ROWS)
    sib_p = pl.multiple_of(512 - core * 512, 512)
    sib_r = pl.multiple_of(PKEYS + ROWS - core * ROWS, ROWS)

    def kv_pieces():
        pieces = []
        for h in range(2):
            cols = pl.ds(HD * h, HD)
            pieces.append((pk_hbm.at[:, cols], kbuf.at[h, pl.ds(own_p, 512)]))
            pieces.append((pv_hbm.at[:, cols], vbuf.at[h, pl.ds(own_p, 512)]))
            pieces.append((rk_hbm.at[:, cols], kbuf.at[h, pl.ds(own_r, ROWS)]))
            pieces.append((rv_hbm.at[:, cols], vbuf.at[h, pl.ds(own_r, ROWS)]))
        return pieces

    def kv_landing():
        places = []
        for h in range(2):
            places.append(kbuf.at[h, pl.ds(sib_p, 512)])
            places.append(vbuf.at[h, pl.ds(sib_p, 512)])
            places.append(kbuf.at[h, pl.ds(sib_r, ROWS)])
            places.append(vbuf.at[h, pl.ds(sib_r, ROWS)])
        return places

    barrier = pltpu.get_barrier_semaphore()

    for s in range(1, CHIPS):
        pl.semaphore_signal(barrier, inc=1, device_id=at(s // NY, s % NY), device_id_type=MESH)
    for dz in range(1, NZ):
        pl.semaphore_signal(barrier, inc=1, device_id=(c, lax.rem(z + dz, NZ)), device_id_type=MESH)
    pl.semaphore_signal(barrier, inc=1, device_id=(sibling, z), device_id_type=MESH)

    q_loads = []
    for h in range(2):
        for g in range(2):
            q_loads.append(pltpu.make_async_copy(
                q_hbm.at[:, pl.ds((2 * h + g) * HD, HD)], qall.at[h, 0, pl.ds(g * ROWS, ROWS)], q_l.at[2 * h + g]))
    dh_load = pltpu.make_async_copy(dh_hbm, dhown, dh_l)
    ow_load = pltpu.make_async_copy(ow_hbm, ow, ow_l)
    for copy in q_loads:
        copy.start()
    dh_load.start()
    for n, (src, dst) in enumerate(kv_pieces()):
        pltpu.make_async_copy(src, dst, kv_l.at[n]).start()
    ow_load.start()
    dkacc[...] = jnp.zeros_like(dkacc)
    dvacc[...] = jnp.zeros_like(dvacc)
    dh_load.wait()
    dh_own = dhown[...].astype(F32)
    for half in range(2):
        dhg[2 * z + half] = dh_own[:, half * JCOLS:(half + 1) * JCOLS].astype(BF16)
    for copy in q_loads:
        copy.wait()
    pl.semaphore_wait(barrier, CHIPS - 1 + NZ - 1 + 1)

    def z_at(dz):
        return lax.rem(z + dz + NZ, NZ)

    def chain(k):
        copies = []
        for way, sems_at in ((1, zu_s), (-1, zd_s)):
            src = z_at(-way * k)
            if k < 3:
                block, sem = dhg.at[pl.ds(2 * src, 2)], zg_r.at[src]
            elif way == 1:
                block, sem = dhg.at[pl.ds(2 * src, 1)], zg_r.at[src]
            else:
                block, sem = dhg.at[pl.ds(2 * src + 1, 1)], zg_r.at[NZ + src]
            copies.append(remote(block, block, sems_at.at[k], sem, (c, z_at(way))))
        return copies

    def chain_arrived(k):
        for way, sems_at in ((1, zu_s), (-1, zd_s)):
            src = z_at(-way * k)
            if k < 4:
                block, sem = dhg.at[pl.ds(2 * src, 2)], zg_r.at[src]
            elif way == 1:
                block, sem = dhg.at[pl.ds(2 * src, 1)], zg_r.at[src]
            else:
                block, sem = dhg.at[pl.ds(2 * src + 1, 1)], zg_r.at[NZ + src]
            remote(block, block, sems_at.at[0], sem, (c, z_at(way))).wait_recv()

    def chain_start(k):
        for copy in chain(k):
            copy.start()

    gather(qall, q_s, q_r, 0)
    chain_start(0)
    for n, (src, dst) in enumerate(kv_pieces()):
        remote(src, dst, kv_s.at[n], kv_r.at[n], (sibling, z)).start()

    for n, (src, dst) in enumerate(kv_pieces()):
        pltpu.make_async_copy(src, dst, kv_l.at[n]).wait()
    for n, dst in enumerate(kv_landing()):
        remote(dst, dst, kv_s.at[n], kv_r.at[n], (sibling, z)).wait_recv()
    for h in range(2):
        vT[h, HD:, :] = jnp.ones((16, KEYS), BF16)
        for n in range(KEYS // HD):
            rows = pl.ds(n * HD, HD)
            kT[h, :, rows] = transpose(kbuf[h, rows, :])
            vT[h, 0:HD, rows] = transpose(vbuf[h, rows, :])
    for stage in (1, 2, 3):
        gather(qall, q_s, q_r, stage)

    def major(i):
        return lax.rem(lax.div(i + 1, 2), NX)

    def first_n(i):
        return 2 * lax.rem(i, 2)

    sub = lax.broadcasted_iota(jnp.int32, (CHUNK, 2 * HD), 0)
    lanes_at = lax.broadcasted_iota(jnp.int32, (1, 2 * HD), 1)

    def weigh(s, mask):
        t = jnp.tanh(s * TANH_IN)
        w = jnp.exp2(t * EXP_IN)
        w = jnp.where(mask, w, 0.0)
        return w.astype(BF16), (w * (1.0 - t * t)).astype(BF16)

    def totals_tail(tot):
        rest = tot - tot.astype(BF16).astype(F32)
        row = lax.broadcasted_iota(jnp.int32, tot.shape, 0)
        return jnp.where(row < 8, tot, rest).astype(BF16)

    def emit_o(i, h, acc):
        tail = totals_tail(acc[HD:, :])
        head = acc[:HD, :].astype(BF16)
        for e in range(2):
            lanes = slice(e * HD, (e + 1) * HD)
            osend[h, major(i), first_n(i) + e, 0:HD, :] = head[:, lanes]
            osend[h, major(i), first_n(i) + e, HD:, :] = tail[:, lanes]

    def wait_gathered(i, buf, send, recv):
        slot = NY * major(i) + first_n(i)

        @pl.when(lax.rem(i, 2) == 1)
        def _():
            for h in range(2):
                arrived(buf, send, recv, h, slot)

        for h in range(2):
            arrived(buf, send, recv, h, slot + 1)

    def at_step(i, k, work):
        @pl.when(i == k)
        def _():
            work()

    def resp_step(i, h):
        return (lax.rem(i, 7) == 0, lax.div(i, 7)) if h == 0 else (lax.rem(i, 2) == 0, lax.div(i, 2))

    position = y * RKEYS + core * ROWS

    def chain_on(k):
        chain_arrived(k)
        chain_start(k)

    def project():
        chain_arrived(4)
        for j in range(CHIPS):
            dfull[:, j * JCOLS:(j + 1) * JCOLS] = dhg[j].astype(F32)
        ow_load.wait()
        grad = dot_nt(dfull[...].astype(BF16), ow[...])
        row_at = lax.broadcasted_iota(jnp.int32, (ROWS, QCOLS), 0) + position
        grad = jnp.where(row_at < len_ref[x], grad, 0.0).astype(BF16)
        for h in range(2):
            for g in range(2):
                doall[h, 0, g * ROWS:(g + 1) * ROWS, :] = grad[:, (2 * h + g) * HD:(2 * h + g + 1) * HD]
        gather(doall, do_s, do_r, 0)

    def forward_step(i, carry):
        m, n0 = major(i), first_n(i)
        at_step(i, 1, lambda: chain_on(1))
        at_step(i, 3, lambda: chain_on(2))
        at_step(i, 5, lambda: chain_on(3))
        at_step(i, 7, project)
        wait_gathered(i, qall, q_s, q_r)
        for h in range(2):
            if h == 0:
                low = high = off_ref[lax.rem(x + m, NX)] - chip * PKEYS
            else:
                low = off_ref[lax.rem(x + n0, NX)] - chip * PKEYS
                high = off_ref[lax.rem(x + n0 + 1, NX)] - chip * PKEYS
            limit = jnp.where(lanes_at < HD, low, high)
            q2 = qall[h, pl.ds(NY * m + n0, 2)].reshape(2 * HD, HD)
            acc = jnp.zeros((HD + 16, 2 * HD), F32)
            for n in range(PKEYS // CHUNK):
                rows = slice(n * CHUNK, (n + 1) * CHUNK)
                wb, gb = weigh(dot_nt(kbuf[h, rows, :], q2), sub < limit - n * CHUNK)
                wbuf[i, h, rows, :] = wb
                gbuf[i, h, rows, :] = gb
                acc = acc + dot_nn(vT[h, :, rows], wb)
            oacc[h] = acc

        for h in range(2):
            has_resp, slot = resp_step(i, h)

            @pl.when(has_resp)
            def _():
                lane = lax.broadcasted_iota(jnp.int32, (RKEYS, 2 * HD), 1)
                key = lax.broadcasted_iota(jnp.int32, (RKEYS, 2 * HD), 0) + y * RKEYS
                row = lax.rem(lane, ROWS) + core * ROWS
                if h == 0:
                    first = lax.rem(y + n0, NY) * RKEYS
                    second = lax.rem(y + n0 + 1, NY) * RKEYS
                    mask = key <= row + jnp.where(lane < HD, first, second)
                else:
                    mask = (key <= row + lax.rem(y + m, NY) * RKEYS) & (lane < HD)
                mask = mask & (key < len_ref[x])
                q2 = qall[h, pl.ds(NY * m + n0, 2)].reshape(2 * HD, HD)
                wb, gb = weigh(dot_nt(kbuf[h, PKEYS:, :], q2), mask)
                wresp[h, slot] = wb
                gresp[h, slot] = gb
                oacc[h] = oacc[h] + dot_nn(vT[h, :, PKEYS:], wb)

        for h in range(2):
            emit_o(i, h, oacc[h])

        @pl.when((lax.rem(i, 2) == 0) & (i > 0))
        def _():
            for h in range(2):
                sum_first(osend, orecv, o1_s, o1_r, h, m).start()

        return carry

    lax.fori_loop(0, PAIRS, forward_step, 0)

    def first_sum(src, first, send, recv, h, n):
        total = src[h, 0, n].astype(F32)
        for m in range(1, NX):
            total = total + first[h, m, n].astype(F32)
        return total

    def last_sum(mid, last, h):
        total = mid[h, 0].astype(F32)
        for n in range(1, NX):
            total = total + last[h, n].astype(F32)
        return total

    for h in range(2):
        for m in range(1, NX):
            sum_arrived(orecv, o1_s, o1_r, h, m)
        for n in (1, 2, 3, 0):
            total = first_sum(osend, orecv, o1_s, o1_r, h, n)
            tot = total[HD:HD + 8, :] + total[HD + 8:, :]
            osum[h, n, 0:HD, :] = total[:HD, :].astype(BF16)
            osum[h, n, HD:, :] = totals_tail(jnp.concatenate([tot, tot], axis=0))
            if n:
                sum_second(osum, olast, o2_s, o2_r, h, n).start()

    lane = lax.broadcasted_iota(jnp.int32, (HD, HD), 1)
    valid = lax.rem(lane, ROWS) + position < len_ref[x]
    stall[0] = jnp.zeros((8, HD), F32)
    for h in range(2):
        for n in range(1, NX):
            sum_arrived(olast, o2_s, o2_r, h, n)
        merged = last_sum(osum, olast, h)
        inv = 1.0 / (merged[HD:HD + 1, :] + merged[HD + 8:HD + 9, :])
        own = jnp.where(valid, merged[0:HD, :] * inv, 0.0).astype(BF16).astype(F32)
        grad_t = transpose(doall[h, 0].astype(F32))
        delta = jnp.sum(own * grad_t, axis=0, keepdims=True)
        stall[0, 2 * h:2 * h + 1, :] = inv
        stall[0, 2 * h + 1:2 * h + 2, :] = delta * inv
        rows_first = transpose(own).astype(BF16)
        for g in range(2):
            atall[h, 0, :, g * HD:(g + 1) * HD] = rows_first[g * ROWS:(g + 1) * ROWS, :]

    def direct(src, buf, send, recv, s):
        dx, dy = s // NY, s % NY
        return remote(src, buf.at[NY * inverse(dx) + inverse(dy)], send, recv, at(dx, dy))

    def direct_all(buf, send, recv):
        blocks = buf.at[pl.ds(1, CHIPS - 1)]
        return remote(blocks, blocks, send, recv, (sibling, z))

    def dh_block(s):
        j = xs[s // NY] * NY + ys[s % NY]
        return dhg.at[j]

    for s in range(1, CHIPS):
        direct(stall.at[0], stall, st_s, st_r, s).start()
    for stage in (1, 2, 3):
        gather(doall, do_s, do_r, stage)
    for h in range(2):
        attn_vm[:, h * 2 * HD:(h + 1) * 2 * HD] = atall[h, 0]
    leave(0)

    def send_dh2():
        for s in range(1, CHIPS):
            direct(dh_block(s), dhall, dh_s, dh_r, s).start()

    hp[...] = dot_nn(attn_vm[...], ow[...])
    for n in range(NZ):
        hsend[n] = hp[:, n * ZCOLS:(n + 1) * ZCOLS].astype(BF16)

    def send_h(dz, carry):
        z_copy(hsend.at[lax.rem(z + dz, NZ)], hrecv.at[z], h_s, h_r, dz).start()
        return carry

    lax.fori_loop(1, NZ, send_h, 0)

    direct_all(stall, st_s, st_r).wait_recv()

    def scaled_grad(i, h):
        m, n0 = major(i), first_n(i)
        parts, deltas = [], []
        for e in range(2):
            stats = stall[NY * m + n0 + e] if h == 0 else stall[NY * (n0 + e) + m]
            inv = transpose(jnp.broadcast_to(stats[2 * h:2 * h + 1, :], (HD, HD)))
            parts.append((doall[h, NY * m + n0 + e].astype(F32) * inv).astype(BF16))
            deltas.append(stats[2 * h + 1:2 * h + 2, :])
        return jnp.concatenate(parts, axis=0), jnp.concatenate(deltas, axis=1)

    def back_chunk(h, rows, wb, gb, q2, do2, delta):
        dp = dot_nt(vbuf[h, rows, :], do2)
        ds = (gb.astype(F32) * (dp - delta)).astype(BF16)
        dkacc[h, rows, :] += dot_nn(ds, q2)
        dvacc[h, rows, :] += dot_nn(wb, do2)
        return dot_nn(kT[h, :, rows], ds)

    def backward_step(t, carry):
        i = lax.rem(t + 1, PAIRS)
        at_step(t, 0, lambda: gather(atall, at_s, at_r, 0))
        at_step(t, 2, send_dh2)
        for stage in (1, 2, 3):
            at_step(t, 2 + stage, lambda stage=stage: gather(atall, at_s, at_r, stage))
        m, n0 = major(i), first_n(i)
        wait_gathered(i, doall, do_s, do_r)
        for h in range(2):
            q2 = qall[h, pl.ds(NY * m + n0, 2)].reshape(2 * HD, HD)
            do2, delta = scaled_grad(i, h)
            acc = jnp.zeros((HD, 2 * HD), F32)
            for n in range(PKEYS // CHUNK):
                rows = slice(n * CHUNK, (n + 1) * CHUNK)
                acc = acc + back_chunk(h, rows, wbuf[i, h, rows, :], gbuf[i, h, rows, :], q2, do2, delta)
            dqacc[h] = acc

        for h in range(2):
            has_resp, slot = resp_step(i, h)

            @pl.when(has_resp)
            def _():
                q2 = qall[h, pl.ds(NY * m + n0, 2)].reshape(2 * HD, HD)
                do2, delta = scaled_grad(i, h)
                dqacc[h] = dqacc[h] + back_chunk(
                    h, slice(PKEYS, KEYS), wresp[h, slot], gresp[h, slot], q2, do2, delta)

        for h in range(2):
            for e in range(2):
                dqsend[h, m, n0 + e] = dqacc[h, :, e * HD:(e + 1) * HD].astype(BF16)

        @pl.when((lax.rem(i, 2) == 0) & (i > 0))
        def _():
            for h in range(2):
                sum_first(dqsend, dqrecv, dq1_s, dq1_r, h, m).start()

        return carry

    lax.fori_loop(0, PAIRS, backward_step, 0)

    def grad_swap(n):
        return remote(gsend.at[n], grecv.at[n], g_s.at[n], g_r.at[n], (sibling, z))

    for n, (acc, scale) in enumerate(((dkacc, 1.0 / 12.0), (dvacc, 1.0))):
        for h in range(2):
            gsend[2 * n + h, 0:512, :] = (acc[h, pl.ds(sib_p, 512), :] * scale).astype(BF16)
            gsend[2 * n + h, 512:, :] = (acc[h, pl.ds(sib_r, ROWS), :] * scale).astype(BF16)
            grad_swap(2 * n + h).start()

    for h in range(2):
        for m in range(1, NX):
            sum_arrived(dqrecv, dq1_s, dq1_r, h, m)
        for n in (1, 2, 3, 0):
            dqsum[h, n] = first_sum(dqsend, dqrecv, dq1_s, dq1_r, h, n).astype(BF16)
            if n:
                sum_second(dqsum, dqlast, dq2_s, dq2_r, h, n).start()

    dhall[0] = dhg[chip]

    direct_all(dhall, dh_s, dh_r).wait_recv()
    for h in range(2):
        for m in range(NX):
            for n in range(1, NX):
                arrived(atall, at_s, at_r, h, NY * m + n)
    for h in range(2):
        blocks = []
        for m in range(NX):
            for n in range(NX):
                blocks.append(dhall[NY * m + n] if h == 0 else dhall[NY * n + m])
        features = jnp.concatenate(blocks, axis=0)
        cols = slice(h * 2 * HD, (h + 1) * 2 * HD)
        part = dot_tn(features, atall[h].reshape(CHIPS * ROWS, 2 * HD))
        low, high = part[:DCOLS, :], part[DCOLS:, :]
        dowsend[:, cols] = jnp.where(core == 0, high, low)
        dow_vm[:, cols] = jnp.where(core == 0, low, high)
    dow_swap = remote(dowsend, dowrecv, dw_s, dw_r, (sibling, z))
    dow_swap.start()

    def add_hidden(dz, total):
        src = lax.rem(z + dz, NZ)
        remote(hsend.at[src], hrecv.at[src], h_s.at[dz], h_r.at[src], (c, src)).wait_recv()
        return total + hrecv[src].astype(F32)

    hidden_vm[...] = lax.fori_loop(1, NZ, add_hidden, hsend[z].astype(F32)).astype(BF16)

    leave(1)

    for n, (acc, scale, prompt_out, resp_out) in enumerate(
        ((dkacc, 1.0 / 12.0, dpk_vm, drk_vm), (dvacc, 1.0, dpv_vm, drv_vm))):
        for h in range(2):
            grad_swap(2 * n + h).wait()
            cols = slice(h * HD, (h + 1) * HD)
            prompt_out[:, cols] = (
                acc[h, pl.ds(own_p, 512), :] * scale + grecv[2 * n + h, 0:512, :].astype(F32)).astype(BF16)
            resp_out[:, cols] = (
                acc[h, pl.ds(own_r, ROWS), :] * scale + grecv[2 * n + h, 512:, :].astype(F32)).astype(BF16)
        leave(3 + n)
        leave(5 + n)

    for h in range(2):
        for n in range(1, NX):
            sum_arrived(dqlast, dq2_s, dq2_r, h, n)
        rows_first = transpose(last_sum(dqsum, dqlast, h) * (1.0 / 12.0)).astype(BF16)
        for g in range(2):
            dq_vm[:, (2 * h + g) * HD:(2 * h + g + 1) * HD] = rows_first[g * ROWS:(g + 1) * ROWS, :]

    leave(2)
    dow_swap.wait()
    dow_vm[...] += dowrecv[...]
    leave(7)

    gather_sent(qall, q_s, q_r)
    gather_sent(doall, do_s, do_r)
    gather_sent(atall, at_s, at_r)
    sum_sent(osend, osum, o1_s, o1_r, o2_s, o2_r)
    sum_sent(dqsend, dqsum, dq1_s, dq1_r, dq2_s, dq2_r)

    direct_all(stall, st_s, st_r).wait_send()
    direct_all(dhall, dh_s, dh_r).wait_send()

    def finish_z(dz, carry):
        z_copy(hsend.at[lax.rem(z + dz, NZ)], hrecv.at[z], h_s, h_r, dz).wait_send()
        return carry

    lax.fori_loop(1, NZ, finish_z, 0)
    for k in range(4):
        for copy in chain(k):
            copy.wait_send()
    for n, (src, dst) in enumerate(kv_pieces()):
        remote(src, dst, kv_s.at[n], kv_r.at[n], (sibling, z)).wait_send()
    for n in range(8):
        leaving(n).wait()


def pass_on(*refs):
    for source, target in zip(refs[:8], refs[8:]):
        target[...] = source[...]


def per_device(resp_query, resp_key, resp_value, prompt_key, prompt_value, o_weight, d_hidden,
               prompt_offsets, resp_lengths):
    smem = pl.BlockSpec(memory_space=pltpu.SMEM)
    vmem = pl.BlockSpec(memory_space=pltpu.VMEM)
    hbm = pl.BlockSpec(memory_space=pl.ANY)
    shape = jax.ShapeDtypeStruct
    sems = pltpu.SemaphoreType.DMA
    plane = (NX, NY)
    out_shape = (
        shape((ROWS, QCOLS), BF16), shape((ROWS, ZCOLS), BF16), shape((ROWS, QCOLS), BF16),
        shape((512, 2 * HD), BF16), shape((512, 2 * HD), BF16),
        shape((ROWS, 2 * HD), BF16), shape((ROWS, 2 * HD), BF16), shape((DCOLS, QCOLS), F32))
    results = pl.pallas_call(
        kernel,
        out_shape=out_shape,
        in_specs=[smem, smem, hbm, hbm, hbm, hbm, hbm, hbm, hbm],
        out_specs=[hbm] * 8,
        scratch_shapes=[pltpu.VMEM(o.shape, o.dtype) for o in out_shape] + [
            pltpu.VMEM((2, CHIPS, HD, HD), BF16),
            pltpu.VMEM((2, CHIPS, HD, HD), BF16),
            pltpu.VMEM((2, KEYS, HD), BF16),
            pltpu.VMEM((2, KEYS, HD), BF16),
            pltpu.VMEM((2, HD, KEYS), BF16),
            pltpu.VMEM((2, HD + 16, KEYS), BF16),
            pltpu.VMEM((PAIRS, 2, PKEYS, 2 * HD), BF16),
            pltpu.VMEM((PAIRS, 2, PKEYS, 2 * HD), BF16),
            pltpu.VMEM((2, 4, RKEYS, 2 * HD), BF16),
            pltpu.VMEM((2, 4, RKEYS, 2 * HD), BF16),
            pltpu.VMEM((2,) + plane + (HD + 16, HD), BF16),
            pltpu.VMEM((2,) + plane + (HD + 16, HD), BF16),
            pltpu.VMEM((2, NX, HD + 16, HD), BF16),
            pltpu.VMEM((2, NX, HD + 16, HD), BF16),
            pltpu.VMEM((CHIPS, 8, HD), F32),
            pltpu.VMEM((2, CHIPS, ROWS, 2 * HD), BF16),
            pltpu.VMEM((CHIPS, ROWS, JCOLS), BF16),
            pltpu.VMEM((ROWS, WIDTH), F32),
            pltpu.VMEM((CHIPS, ROWS, JCOLS), BF16),
            pltpu.VMEM((QCOLS, WIDTH), BF16),
            pltpu.VMEM((ROWS, WIDTH), F32),
            pltpu.VMEM((NZ, ROWS, ZCOLS), BF16),
            pltpu.VMEM((NZ, ROWS, ZCOLS), BF16),
            pltpu.VMEM((2,) + plane + (HD, HD), BF16),
            pltpu.VMEM((2,) + plane + (HD, HD), BF16),
            pltpu.VMEM((2, NX, HD, HD), BF16),
            pltpu.VMEM((2, NX, HD, HD), BF16),
            pltpu.VMEM((2, KEYS, HD), F32),
            pltpu.VMEM((2, KEYS, HD), F32),
            pltpu.VMEM((4, KEYS // 2, HD), BF16),
            pltpu.VMEM((4, KEYS // 2, HD), BF16),
            pltpu.VMEM((DCOLS, QCOLS), F32),
            pltpu.VMEM((DCOLS, QCOLS), F32),
            pltpu.VMEM((2, HD + 16, 2 * HD), F32),
            pltpu.VMEM((2, HD, 2 * HD), F32),
            pltpu.VMEM((ROWS, ZCOLS), BF16),
        ] + [sems, sems((2, CHIPS))] * 3 + [sems, sems] + [sems, sems((2, NX))] * 4 + [sems, sems] + [
            sems((4,)), sems((4,)), sems((2 * NZ,)), sems((NZ,)), sems((NZ,)), sems((4,)), sems, sems((8,)), sems((8,)), sems((8,)), sems, sems((4,)), sems((4,)), sems, sems, sems((8,))],
        compiler_params=pltpu.CompilerParams(
            collective_id=0, has_side_effects=True, vmem_limit_bytes=56 * 1024 * 1024),
        cost_estimate=pl.CostEstimate(flops=10 ** 10, bytes_accessed=10 ** 7, transcendentals=10 ** 7),
    )(prompt_offsets, resp_lengths, resp_query, d_hidden, resp_key, resp_value, prompt_key, prompt_value, o_weight)
    results = pl.pallas_call(
        pass_on, out_shape=out_shape, in_specs=[vmem] * 8, out_specs=[vmem] * 8)(*results)
    return results[:7] + (results[7].T,)


def solution(mesh):
    both = P("ctx", "tp")
    return jax.shard_map(
        per_device, mesh=mesh,
        in_specs=(both, both, both, both, both, P("tp", None), both, P(), P()),
        out_specs=(both, both, both, both, both, both, both, P("tp", "ctx")),
        check_vma=False)
```
